256 devices in a mesh: tm: 4 (over y), tile: 64 (over z, x, core).
Axes of the slice: x: 4, y: 4, z: 8, core: 2. Of those that a mesh axis runs over, the one named last changes fastest.
Arguments:
- latent: bfloat16 [8, 128, 128, 512], P('tm', 'tile'), may hold values from -90 to 90
- kernel: bfloat16 [512, 3, 3, 3, 512], P(('tm', 'tile')), may hold values from -0.0546875 to 0.0546875
- norm_gain: float32 [512], replicated, may hold values from 0.5 to 2
- norm_shift: float32 [512], replicated, may hold values from -3 to 3
- conv_bias: float32 [512], replicated, may hold values from -3 to 3
Outputs:
- decoded: bfloat16 [8, 128, 128, 512], P('tm', 'tile')
The draws below stay inside these ranges and needn't reach their ends.
All inputs are finite; a program needn't handle non-finite values.
Results may differ from the reference program's by a relative error of at most 0.0044.
The reference program's roundings to bfloat16 on the way (of `active`) count: a program that leaves them out, or rounds other values in their place, can miss the bound.
Values may be sent and summed in bfloat16 or wider, within the bound.
No kernel may reach another device: no remote copies, remote signals or barrier semaphores. Data moves between devices by JAX's collectives and lax.ppermute only.
A program may use at most 128 MiB of HBM per device.

```python
import math
import jax
import jax.numpy as jnp
from jax import lax

C = 512
GROUPS = 32
FRAMES_DEV = 2
WIDTH = 128
FRAMES = 8
HEIGHT = 128
N_TM = 4


def draw_latent(key, part):
    key = jax.random.fold_in(key, 11)
    key_noise, key_rough, key_channel = jax.random.split(key, 3)
    row_pos = jnp.arange(HEIGHT, dtype=jnp.float32) / max(HEIGHT - 1, 1)
    roughness = jnp.exp(jax.random.uniform(key_rough, (FRAMES, HEIGHT, 1, 1), jnp.float32, 0.0, math.log(2.0)))
    channel_scale = jnp.exp(jax.random.uniform(key_channel, (C,), jnp.float32, math.log(0.3), math.log(3.0)))
    trend = jnp.exp(math.log(10.0) * row_pos)
    noise = jnp.clip(jax.random.normal(key_noise, (FRAMES, HEIGHT, WIDTH, C), jnp.float32), -6.0, 6.0)
    values = 0.25 * noise * trend[None, :, None, None] * roughness * channel_scale
    return values.astype(jnp.bfloat16)


def block_scale(stream_key, extent, shards, low, largest):
    gain = 1.0
    for axis_at, blocks in shards:
        steps = jax.random.uniform(jax.random.fold_in(jax.random.fold_in(stream_key, 6), axis_at), (blocks,), jnp.float32, low / len(shards), largest / len(shards))
        gain = gain * jnp.repeat(jnp.exp(steps), extent[axis_at] // blocks).reshape((-1,) + (1,) * (len(extent) - 1 - axis_at))
    return gain


def normal_values(key, dims, width, limit, shards=(), kind=jnp.bfloat16):
    factor_of = block_scale(key, dims, shards, -0.22, 0.18) if shards else 1.0
    drawn = jax.random.normal(key, dims, jnp.float32) * width * factor_of
    return jnp.minimum(jnp.maximum(drawn, -limit), limit).astype(kind)


def setup_inputs(seed: int = 0) -> dict:
    key_list = jax.random.split(jax.random.key(seed), 6)
    return {
        "latent": draw_latent(jax.random.fold_in(key_list[5], 71), 0),
        "kernel": normal_values(key_list[1], (C, 3, 3, 3, C), (27 * C) ** -0.5, 0.0546875, ((0, 256),)),
        "norm_gain": jnp.clip(jnp.exp(jax.random.uniform(key_list[2], (C,), jnp.float32, math.log(0.5), math.log(2.0))), 0.5, 2.0),
        "norm_shift": normal_values(key_list[3], (C,), 0.5, 3.0, (), jnp.float32),
        "conv_bias": normal_values(key_list[4], (C,), 0.5, 3.0, (), jnp.float32),
    }


def normalize_span(span, norm_gain, norm_shift):
    cell_count = span.shape[0] * span.shape[1] * span.shape[2]
    grouped = span.astype(jnp.float32).reshape(cell_count, GROUPS, C // GROUPS)
    group_mean = lax.optimization_barrier(jnp.mean(grouped, axis=(0, 2)))
    centered = grouped - group_mean[None, :, None]
    variance = lax.optimization_barrier(jnp.mean(centered * centered, axis=(0, 2)))
    scaled = (centered * lax.rsqrt(variance + 1e-06)[None, :, None]).reshape(span.shape)
    return jax.nn.silu(scaled * norm_gain + norm_shift).astype(jnp.bfloat16)

def reference(latent, kernel, norm_gain, norm_shift, conv_bias):
    spans = latent.reshape(N_TM, FRAMES_DEV, HEIGHT, WIDTH, C)

    def per_span(span):
        return normalize_span(span, norm_gain, norm_shift)
    active = lax.map(per_span, spans).reshape(FRAMES, HEIGHT, WIDTH, C)
    opening = active[:1]
    padded = jnp.concatenate([opening, opening, active], axis=0)
    padded = jnp.pad(padded, ((0, 0), (1, 1), (1, 1), (0, 0)))

    def one_frame(frame_index):
        window = lax.dynamic_slice_in_dim(padded, frame_index, 3, 0)
        summed = jnp.zeros((HEIGHT * WIDTH, C), jnp.float32)
        for time_tap in range(3):
            for row_tap in range(3):
                for col_tap in range(3):
                    sliced = window[time_tap, row_tap:row_tap + HEIGHT, col_tap:col_tap + WIDTH, :]
                    sliced = sliced.reshape(HEIGHT * WIDTH, C)
                    summed = summed + jnp.dot(sliced, kernel[:, time_tap, row_tap, col_tap, :].T, preferred_element_type=jnp.float32)
        return (summed + conv_bias).astype(jnp.bfloat16).reshape(HEIGHT, WIDTH, C)
    return lax.map(one_frame, jnp.arange(FRAMES, dtype=jnp.int32))
```

```python
import jax
import jax.numpy as jnp
from jax import lax
from jax.experimental import pallas as pl
from jax.experimental.pallas import tpu as pltpu
from jax.sharding import PartitionSpec as P

GROUPS = 32
EPSILON = 1e-06
NY, NZ, NX, NC = 4, 8, 4, 2
DEVICES = NY * NZ * NX * NC
AXES = ("tm", "tile")
FRAMES, ROWS, WIDTH, HALF, OUTS = 8, 4, 128, 256, 128
VMEM = 56 * 2**20


def send(array, move):
    pairs = []
    for y in range(NY):
        for z in range(NZ):
            for x in range(NX):
                for c in range(NC):
                    to = move(y, z, x, c)
                    if to is not None:
                        ty, tz, tx, tc = to
                        source = ((y * NZ + z) * NX + x) * NC + c
                        target = ((ty % NY * NZ + tz % NZ) * NX + tx % NX) * NC + tc % NC
                        pairs.append((source, target))
    return lax.ppermute(array, AXES, pairs)


def along_y(by):
    return lambda y, z, x, c: (y + by, z, x, c)


def along_z(by):
    return lambda y, z, x, c: (y, z + by, x, c)


def along_x(by):
    return lambda y, z, x, c: (y, z, x + by, c)


def sibling(y, z, x, c):
    return (y, z, x, 1 - c)


def strip(by):
    def move(y, z, x, c):
        chip = z * NX + x + by
        return (y, chip // NX, chip % NX, c) if 0 <= chip < NZ * NX else None
    return move


def conv_kernel(info, stat, own, after, across_a, across_b, before, *rest):
    weights, (keep, give, act, taps) = rest[:NZ], rest[NZ:]
    time_index, plane, top, bottom, core = (info[i] for i in range(5))
    column = lax.broadcasted_iota(jnp.int32, (WIDTH, HALF), 0)
    for j in range(NZ):
        taps[:, lax.rem(plane + j, NZ)] = weights[j][...]
    pieces = ((own, 0, 0, 2), (after, 1, 0, 2), (across_a, 2, 0, 1), (across_b, 2, 1, 1), (before, 3, 0, 2))
    for piece, ahead, first, count in pieces:
        span = lax.rem(time_index + ahead, NY)
        mean, gain, shift = (stat[span, i : i + 1] for i in range(3))

        def row(i, _):
            frame, r = i // 6, lax.rem(i, 6)
            v = (piece[frame, r].astype(jnp.float32) - mean) * gain + shift
            s = v / (1.0 + jnp.exp(-v))
            inside = jnp.logical_and(
                jnp.logical_or(r != 0, top == 0), jnp.logical_or(r != 5, bottom == 0)
            )
            s = jnp.where(inside, s, 0.0)
            at = 2 * span + first + frame
            act[1, at, r] = s.astype(jnp.bfloat16)
            act[0, at, r] = jnp.where(column == 0, 0.0, pltpu.roll(s, 1, 0)).astype(jnp.bfloat16)
            act[2, at, r] = jnp.where(column == WIDTH - 1, 0.0, pltpu.roll(s, WIDTH - 1, 0)).astype(jnp.bfloat16)
            return 0

        lax.fori_loop(0, 6 * count, row, 0, unroll=2)

    def products(frame):
        total = None
        for b in range(3):
            for c in range(3):
                lhs = act[c, frame, b : b + ROWS].reshape(ROWS * WIDTH, HALF)
                rhs = jnp.concatenate([taps[(a * 3 + b) * 3 + c].reshape(OUTS, HALF) for a in range(3)], 0)
                term = lax.dot_general(lhs, rhs, (((1,), (1,)), ((), ())), preferred_element_type=jnp.float32)
                total = term if total is None else total + term
        return total[:, :OUTS], total[:, OUTS : 2 * OUTS], total[:, 2 * OUTS :]

    def emit(frame, value):
        value = value.reshape(ROWS, WIDTH, OUTS)

        @pl.when(core == 0)
        def _():
            keep[frame] = value[:2]
            give[frame] = value[2:]

        @pl.when(core == 1)
        def _():
            keep[frame] = value[2:]
            give[frame] = value[:2]

    first, second, third = products(0)
    emit(0, first + second + third)

    def step(frame, carry):
        ready, started = carry
        first, second, third = products(frame)
        emit(frame, ready + third)
        return started + second, first

    lax.fori_loop(1, FRAMES, step, (first + second, first))


def convolve(info, stat, pieces, weights):
    vmem = pl.BlockSpec(memory_space=pltpu.VMEM)
    shape = jax.ShapeDtypeStruct((FRAMES, 2, WIDTH, OUTS), jnp.float32)
    return pl.pallas_call(
        conv_kernel,
        out_shape=[shape, shape],
        in_specs=[pl.BlockSpec(memory_space=pltpu.SMEM)] + [vmem] * (1 + len(pieces) + len(weights)),
        out_specs=[vmem, vmem],
        scratch_shapes=[
            pltpu.VMEM((3, FRAMES, ROWS + 2, WIDTH, HALF), jnp.bfloat16),
            pltpu.VMEM((27, NZ, 16, HALF), jnp.bfloat16),
        ],
        compiler_params=pltpu.CompilerParams(vmem_limit_bytes=VMEM),
        cost_estimate=pl.CostEstimate(flops=2 * 4096 * 256 * 27 * 128, bytes_accessed=8 * 2**20, transcendentals=0),
    )(info, stat, *pieces, *weights)


def per_device(latent, kernel, norm_gain, norm_shift, conv_bias):
    time_index = lax.axis_index("tm")
    tile = lax.axis_index("tile")
    plane, core, chip = tile // (NX * NC), tile % NC, tile // NC
    channels = latent.shape[3]
    group_width = channels // GROUPS

    half = lambda a, which: lax.dynamic_slice_in_dim(a, which * HALF, HALF, axis=a.ndim - 1)
    theirs = send(half(latent, 1 - core), sibling)
    mine = half(latent, core)
    rows = jnp.zeros((2, ROWS, WIDTH, HALF), jnp.bfloat16)
    rows = lax.dynamic_update_slice(rows, mine, (0, 2 * core, 0, 0))
    rows = lax.dynamic_update_slice(rows, theirs, (0, 2 - 2 * core, 0, 0))
    above = send(rows[:, ROWS - 1 :], strip(1))
    below = send(rows[:, :1], strip(-1))
    own = jnp.concatenate([above, rows, below], axis=1)
    after = send(own, along_y(-1))
    before = send(own, along_y(1))
    across_a = send(after[:1], along_y(-1))
    across_b = send(before[1:], along_y(1))

    shard = kernel.reshape(2, 27, channels)
    other = send(half(shard, 1 - core), sibling)
    near = half(shard, core)
    pair = jnp.where(core == 0, jnp.stack([near, other]), jnp.stack([other, near]))
    pair = pair.reshape(4, 27, HALF)
    x_index = (tile // NC) % NX
    block = jnp.zeros((NX, 4, 27, HALF), jnp.bfloat16)
    for by in range(NX):
        got = pair if by == 0 else send(pair, along_x(-by))
        block = lax.dynamic_update_slice(block, got[None], ((x_index + by) % NX, 0, 0, 0))
    block = block.reshape(16, 27, HALF).transpose(1, 0, 2)
    ring = [block] + [None] * (NZ - 1)
    for by in range(1, 4):
        ring[by] = send(ring[by - 1], along_z(-1))
        ring[-by] = send(ring[(1 - by) % NZ], along_z(1))
    ring[4] = jnp.concatenate(
        [send(ring[3][:14], along_z(-1)), send(ring[5][14:], along_z(1))], axis=0
    )

    grouped = latent.astype(jnp.float32)
    cells = 2 * 2 * WIDTH * group_width
    local_sum = jnp.sum(jnp.sum(grouped, axis=(0, 1, 2)).reshape(GROUPS, group_width), axis=1)
    local_mean = local_sum / cells
    centered = grouped - jnp.repeat(local_mean, group_width)
    local_squares = jnp.sum(jnp.sum(centered * centered, axis=(0, 1, 2)).reshape(GROUPS, group_width), axis=1)
    local = jnp.concatenate([local_mean, local_squares, jnp.zeros((64,), jnp.float32)])[None]
    everyone = jnp.broadcast_to(local[None], (DEVICES, 1, 128))
    everyone = lax.all_to_all(everyone, AXES, 0, 0).reshape(NY, DEVICES // NY, 128)
    means, squares = everyone[..., :GROUPS], everyone[..., GROUPS : 2 * GROUPS]
    group_mean = jnp.mean(means, axis=1)
    deviation = means - group_mean[:, None]
    variance = (jnp.sum(squares, axis=1) / cells + jnp.sum(deviation * deviation, axis=1)) / (DEVICES // NY)
    inv_spread = lax.rsqrt(variance + EPSILON)
    stat = jnp.stack(
        [
            jnp.repeat(group_mean, group_width, axis=1),
            jnp.repeat(inv_spread, group_width, axis=1) * norm_gain,
            jnp.broadcast_to(norm_shift, (NY, channels)),
        ],
        axis=1,
    )
    stat = half(stat, core)
    info = jnp.stack([time_index, plane, chip == 0, chip == NZ * NX - 1, core]).astype(jnp.int32)

    keep, give = convolve(info, stat, [own, after, across_a, across_b, before], ring)
    bias = lax.dynamic_slice_in_dim(conv_bias, time_index * OUTS, OUTS)
    mixed = (keep + send(give, sibling) + bias).astype(jnp.bfloat16)
    mixed = lax.all_to_all(mixed.reshape(NY, 2, 2, WIDTH, OUTS), "tm", 0, 0)
    return mixed.transpose(1, 2, 3, 0, 4).reshape(2, 2, WIDTH, channels)


def solution(mesh):
    return jax.shard_map(
        per_device,
        mesh=mesh,
        in_specs=(
            P("tm", "tile", None, None),
            P(("tm", "tile"), None, None, None, None),
            P(),
            P(),
            P(),
        ),
        out_specs=P("tm", "tile", None, None),
        check_vma=False,
    )
```

```python
import jax
import jax.numpy as jnp
from jax import lax
from jax.experimental import pallas as pl
from jax.experimental.pallas import tpu as pltpu
from jax.sharding import Mesh, PartitionSpec as P

GROUPS = 32
EPSILON = 1e-06
NY, NZ, NX, NC = 4, 8, 4, 2
CHIPS = NZ * NX
TAPS = 27

AXES = ("y", "z", "x", "core")
FRAMES, ROWS, WIDTH, HALF, OUTS = 8, 4, 128, 256, 128
CELLS = 2 * ROWS * WIDTH * 16
VMEM = pl.BlockSpec(memory_space=pltpu.VMEM)
HBM = pl.BlockSpec(memory_space=pltpu.HBM)
SMEM = pl.BlockSpec(memory_space=pltpu.SMEM)
LIMIT = pltpu.CompilerParams(vmem_limit_bytes=24 * 2**20)


def send(array, move):
    pairs = []
    for y in range(NY):
        for z in range(NZ):
            for x in range(NX):
                for c in range(NC):
                    to = move(y, z, x, c)
                    if to is not None:
                        ty, tz, tx, tc = to
                        source = ((y * NZ + z) * NX + x) * NC + c
                        target = ((ty % NY * NZ + tz % NZ) * NX + tx % NX) * NC + tc % NC
                        pairs.append((source, target))
    return lax.ppermute(array, AXES, pairs)


def along_y(by):
    return lambda y, z, x, c: (y + by, z, x, c)


def along_z(by):
    return lambda y, z, x, c: (y, z + by, x, c)


def along_x(by):
    return lambda y, z, x, c: (y, z, x + by, c)


def sibling(y, z, x, c):
    return (y, z, x, 1 - c)


def strip(by):
    def move(y, z, x, c):
        chip = (z * NX + x + by) % CHIPS
        return (y, chip // NX, chip % NX, c)

    return move


def pack(info, latent, shard):
    def body(info, latent, shard, latent_out, shard_out, sems):
        at = pl.multiple_of((1 - info[4]) * HALF, HALF)
        copies = [
            pltpu.make_async_copy(shard.at[:, :, pl.ds(at, HALF)], shard_out, sems.at[0]),
            pltpu.make_async_copy(latent.at[:, :, :, pl.ds(at, HALF)], latent_out, sems.at[1]),
        ]
        for copy in copies:
            copy.start()
        for copy in copies:
            copy.wait()

    return pl.pallas_call(
        body,
        out_shape=[
            jax.ShapeDtypeStruct(latent.shape[:3] + (HALF,), latent.dtype),
            jax.ShapeDtypeStruct(shard.shape[:2] + (HALF,), shard.dtype),
        ],
        in_specs=[SMEM, HBM, HBM],
        out_specs=[HBM, HBM],
        scratch_shapes=[pltpu.SemaphoreType.DMA((2,))],
        compiler_params=LIMIT,
    )(info, latent, shard)


def unpack(info, latent, theirs):
    def body(info, latent, theirs, rows, last, first, stat, sems):
        core = info[4]
        at = pl.multiple_of(core * HALF, HALF)
        copies = [
            pltpu.make_async_copy(
                latent.at[:, :, :, pl.ds(at, HALF)], rows.at[:, pl.ds(2 * core, 2)], sems.at[0]
            ),
            pltpu.make_async_copy(theirs, rows.at[:, pl.ds(2 - 2 * core, 2)], sems.at[1]),
        ]
        for copy in copies:
            copy.start()
        for copy in copies:
            copy.wait()
        last[...] = rows[:, ROWS - 1 :]
        first[...] = rows[:, :1]
        group = [lax.broadcasted_iota(jnp.int32, (HALF, HALF), i) // 16 for i in range(2)]
        same = (group[0] == group[1]).astype(jnp.float32)

        def over_group(values):
            values = jnp.broadcast_to(jnp.sum(values, axis=0, keepdims=True), (8, HALF))
            return lax.dot_general(
                values, same, (((1,), (0,)), ((), ())), precision=lax.Precision.HIGHEST,
                preferred_element_type=jnp.float32,
            )[:1]

        def total(of):
            sums = None
            for frame in range(2):
                for r in range(ROWS):
                    part = of(rows[frame, r].astype(jnp.float32))
                    part = jnp.sum(part.reshape(WIDTH // 8, 8, HALF), axis=0)
                    sums = part if sums is None else sums + part
            return over_group(sums)

        mean = total(lambda v: v) / CELLS
        squares = total(lambda v: (v - mean) * (v - mean))
        stat[0:1] = mean
        stat[1:2] = squares

    edge = jax.ShapeDtypeStruct((2, 1, WIDTH, HALF), latent.dtype)
    return pl.pallas_call(
        body,
        out_shape=[
            jax.ShapeDtypeStruct((2, ROWS, WIDTH, HALF), latent.dtype), edge, edge,
            jax.ShapeDtypeStruct((2, HALF), jnp.float32),
        ],
        in_specs=[SMEM, HBM, HBM],
        out_specs=[VMEM] * 4,
        scratch_shapes=[pltpu.SemaphoreType.DMA((2,))],
        compiler_params=LIMIT,
    )(info, latent, theirs)


def border(above, rows, below):
    edge = 2 * WIDTH

    def body(above, rows, below, own, sems):
        copies = [pltpu.make_async_copy(rows, own.at[:, pl.ds(1, ROWS)], sems.at[0])]
        for frame in range(2):
            at = pl.ds(frame * WIDTH, WIDTH)
            copies.append(pltpu.make_async_copy(above.at[at], own.at[frame, 0], sems.at[1 + frame]))
            copies.append(pltpu.make_async_copy(below.at[at], own.at[frame, ROWS + 1], sems.at[3 + frame]))
        for copy in copies:
            copy.start()
        for copy in copies:
            copy.wait()

    return pl.pallas_call(
        body,
        out_shape=jax.ShapeDtypeStruct((2, ROWS + 2, WIDTH, HALF), rows.dtype),
        in_specs=[HBM] * 3,
        out_specs=HBM,
        scratch_shapes=[pltpu.SemaphoreType.DMA((5,))],
        compiler_params=LIMIT,
    )(above, rows, below)


def activate(info, stats, gain, shift, pieces):
    def body(info, stats, gain, shift, *refs):
        sources, results = refs[: len(pieces)], refs[len(pieces) :]
        for (_, ahead), source, result in zip(pieces, sources, results):
            means, squares = stats[:, 2 * ahead], stats[:, 2 * ahead + 1]
            mean = jnp.sum(means, axis=0, keepdims=True) / CHIPS
            deviation = means - mean
            variance = jnp.sum(squares / CELLS + deviation * deviation, axis=0, keepdims=True) / CHIPS
            scale = lax.rsqrt(variance + EPSILON) * gain[...]
            offset = shift[...]

            def row(i, _):
                frame, r = i // 6, lax.rem(i, 6)
                v = (source[frame, r].astype(jnp.float32) - mean) * scale + offset
                s = v / (1.0 + jnp.exp(-v))
                inside = jnp.logical_and(
                    jnp.logical_or(r != 0, info[2] == 0), jnp.logical_or(r != 5, info[3] == 0)
                )
                result[frame, r] = jnp.where(inside, s, 0.0).astype(jnp.bfloat16)
                return 0

            lax.fori_loop(0, 6 * source.shape[0], row, 0, unroll=2)

    arrays = [a for a, _ in pieces]
    cells = sum(a.size for a in arrays)
    return pl.pallas_call(
        body,
        out_shape=[jax.ShapeDtypeStruct(a.shape, a.dtype) for a in arrays],
        in_specs=[SMEM] + [VMEM] * (3 + len(arrays)),
        out_specs=[VMEM] * len(arrays),
        compiler_params=LIMIT,
        cost_estimate=pl.CostEstimate(flops=16 * cells, bytes_accessed=4 * cells, transcendentals=2 * cells),
    )(info, stats, gain, shift, *arrays)


def convolve(info, act, chunks, order):
    sizes = [len(piece) for piece in act]

    def body(info, *refs):
        pieces, at = [], 0
        for size in sizes:
            piece = refs[at : at + size]
            pieces.append([(piece[0], 0), (piece[0], 1)] if size == 1 else [(piece[0], 0), (piece[1], 0)])
            at += size
        taps, (keep, give) = refs[at:-2], refs[-2:]
        column = lax.broadcasted_iota(jnp.int32, (1, WIDTH, OUTS), 1)

        def matrix(tap):
            rows = [c[tap] for c in taps[:4]]
            rows.append(jnp.concatenate([taps[4][tap], taps[5][tap]], 1))
            return jnp.concatenate(rows + [c[tap] for c in taps[6:]], 0)

        def run(slot, frames):
            for t in range(2):
                total = None
                for a in range(3):
                    ref, at = frames[t + a]
                    for b in range(3):
                        lhs = ref[at, b : b + ROWS].reshape(ROWS * WIDTH, HALF)
                        rhs = jnp.concatenate([matrix((a * 3 + b) * 3 + c) for c in range(3)], 0)
                        term = lax.dot_general(
                            lhs, rhs, (((1,), (1,)), ((), ())), preferred_element_type=jnp.float32
                        )
                        total = term if total is None else total + term
                total = total.reshape(ROWS, WIDTH, 3 * OUTS)
                left, middle, right = (total[..., c * OUTS : (c + 1) * OUTS] for c in range(3))
                left = jnp.where(column == 0, 0.0, pltpu.roll(left, 1, 1))
                right = jnp.where(column == WIDTH - 1, 0.0, pltpu.roll(right, WIDTH - 1, 1))
                total = pltpu.roll((left + middle + right).reshape(ROWS * WIDTH, OUTS), info[1], 1)
                total = total.reshape(ROWS, WIDTH, OUTS)

                @pl.when(info[4] == 0)
                def _():
                    keep[slot, t] = total[:2]
                    give[slot, t] = total[2:]

                @pl.when(info[4] == 1)
                def _():
                    keep[slot, t] = total[2:]
                    give[slot, t] = total[:2]

        for slot, ahead in enumerate(order):
            now, before = pieces[ahead], pieces[ahead - 1]
            span = lax.rem(info[0] + ahead, NY)

            @pl.when(span == 0)
            def _():
                run(slot, [now[0], now[0]] + now)

            @pl.when(span != 0)
            def _():
                run(slot, before + now)

    shape = jax.ShapeDtypeStruct((len(order), 2, 2, WIDTH, OUTS), jnp.float32)
    arrays = [a for piece in act for a in piece]
    return pl.pallas_call(
        body,
        out_shape=[shape, shape],
        in_specs=[SMEM] + [VMEM] * (len(arrays) + len(chunks)),
        out_specs=[VMEM, VMEM],
        compiler_params=LIMIT,
        cost_estimate=pl.CostEstimate(
            flops=len(order) * 2 * 1024 * HALF * 27 * OUTS, bytes_accessed=5 * 2**20, transcendentals=0
        ),
    )(info, *arrays, *chunks)


def assemble(info, quarters):
    def body(info, *refs):
        out = refs[-1]
        for k in range(NY):
            at = pl.multiple_of(lax.rem(info[0] + k, NY) * OUTS, OUTS)
            out[:, :, :, pl.ds(at, OUTS)] = refs[k][...]

    return pl.pallas_call(
        body,
        out_shape=jax.ShapeDtypeStruct((2, 2, WIDTH, NY * OUTS), jnp.bfloat16),
        in_specs=[SMEM] + [VMEM] * NY,
        out_specs=VMEM,
        compiler_params=LIMIT,
    )(info, *quarters)


def per_device(latent, kernel, norm_gain, norm_shift, conv_bias):
    time_index, plane, x_index, core = (lax.axis_index(a) for a in AXES)
    chip = plane * NX + x_index
    channels = latent.shape[3]
    turn = 4 * ((chip + CHIPS - 1) % CHIPS)
    info = jnp.stack([time_index, turn, chip == 0, chip == CHIPS - 1, core]).astype(jnp.int32)
    half = lambda a: lax.dynamic_slice_in_dim(a, core * HALF, HALF, axis=a.ndim - 1)

    shard = kernel.transpose(1, 2, 3, 0, 4).reshape(TAPS, 2, channels)
    latent_give, shard_give = pack(info, latent, shard)
    other = send(shard_give, sibling)
    theirs = send(latent_give, sibling)

    near = half(shard)
    pair = jnp.where(core == 0, jnp.concatenate([near, other], 1), jnp.concatenate([other, near], 1))
    rows, last, first, stat = unpack(info, latent, theirs)
    flat = pair.reshape(TAPS * 4, HALF)
    edge = 2 * WIDTH
    from_above = send(jnp.concatenate([last.reshape(edge, HALF), flat]), strip(1))
    from_below = send(jnp.concatenate([first.reshape(edge, HALF), flat]), strip(-1))
    from_second = send(pair, strip(-2))
    block = jnp.concatenate(
        [from_above[edge:].reshape(TAPS, 4, HALF), pair, from_below[edge:].reshape(TAPS, 4, HALF), from_second], 1
    )
    own = border(from_above, rows, from_below)

    spans = [stat] + [send(stat, along_y(-k)) for k in range(1, NY)]
    spans = jnp.concatenate(spans, 0)
    spans, block, own = lax.optimization_barrier((spans, block, own))
    stats = lax.all_to_all(jnp.broadcast_to(spans[None], (CHIPS, 2 * NY, HALF)), ("z", "x"), 0, 0)

    ring = {0: block}
    for by in range(1, 4):
        ring[by] = send(ring[by - 1], along_z(-1))
        ring[-by] = send(ring[1 - by], along_z(1))
    after = send(own, along_y(-1))
    before = send(own, along_y(1))
    across_a = send(after[:1], along_y(-1))
    across_b = send(before[1:], along_y(1))

    gain, shift = half(norm_gain[None]), half(norm_shift[None])
    act_own, act_after, act_before = activate(info, stats, gain, shift, [(own, 0), (after, 1), (before, 3)])
    third, minus_third, act_own, act_after, act_before = lax.optimization_barrier(
        (ring[3], ring[-3], act_own, act_after, act_before)
    )
    far_a = send(third[..., :WIDTH], along_z(-1))
    far_b = send(minus_third[..., WIDTH:], along_z(1))
    chunks = [ring[0], ring[1], ring[2], ring[3], far_a, far_b, ring[-3], ring[-2], ring[-1]]
    act_a, act_b = activate(info, stats, gain, shift, [(across_a, 2), (across_b, 2)])
    act = [[act_own], [act_after], [act_a, act_b], [act_before]]
    bias = lax.dynamic_slice_in_dim(conv_bias, time_index * OUTS, OUTS)
    keep, give = convolve(info, act, chunks, range(NY))
    mixed = (keep + send(give, sibling) + bias).astype(jnp.bfloat16)
    quarters = [mixed[0]] + [None] * (NY - 1)
    for ahead in (2, 1, 3):
        quarters[-ahead] = send(mixed[ahead], along_y(ahead))
    return assemble(info, quarters)


def solution(mesh):
    mesh = Mesh(mesh.devices.reshape(NY, NZ, NX, NC), AXES)
    return jax.shard_map(
        per_device,
        mesh=mesh,
        in_specs=(
            P("y", ("z", "x", "core"), None, None),
            P(AXES, None, None, None, None),
            P(),
            P(),
            P(),
        ),
        out_specs=P("y", ("z", "x", "core"), None, None),
        check_vma=False,
    )
```

```python
import jax
import jax.numpy as jnp
from jax import lax
from jax.experimental import pallas as pl
from jax.experimental.pallas import tpu as pltpu
from jax.sharding import Mesh, PartitionSpec as P

GROUPS = 32
EPSILON = 1e-06
NY, NZ, NX, NC = 4, 8, 4, 2
CHIPS = NZ * NX
TAPS = 27

AXES = ("y", "z", "x", "core")
FRAMES, ROWS, WIDTH, HALF, OUTS = 8, 4, 128, 256, 128
CELLS = 2 * ROWS * WIDTH * 16
VMEM = pl.BlockSpec(memory_space=pltpu.VMEM)
HBM = pl.BlockSpec(memory_space=pltpu.HBM)
SMEM = pl.BlockSpec(memory_space=pltpu.SMEM)
LIMIT = pltpu.CompilerParams(vmem_limit_bytes=14 * 2**20)
WIDE = pltpu.CompilerParams(vmem_limit_bytes=60 * 2**20)


def send(array, move):
    pairs = []
    for y in range(NY):
        for z in range(NZ):
            for x in range(NX):
                for c in range(NC):
                    to = move(y, z, x, c)
                    if to is not None:
                        ty, tz, tx, tc = to
                        source = ((y * NZ + z) * NX + x) * NC + c
                        target = ((ty % NY * NZ + tz % NZ) * NX + tx % NX) * NC + tc % NC
                        pairs.append((source, target))
    return lax.ppermute(array, AXES, pairs)


def along_y(by):
    return lambda y, z, x, c: (y + by, z, x, c)


def along_z(by):
    return lambda y, z, x, c: (y, z + by, x, c)


def along_x(by):
    return lambda y, z, x, c: (y, z, x + by, c)


def sibling(y, z, x, c):
    return (y, z, x, 1 - c)


def strip(by):
    def move(y, z, x, c):
        chip = (z * NX + x + by) % CHIPS
        return (y, chip // NX, chip % NX, c)

    return move


def pack(info, latent, shard):
    def body(info, latent, shard, latent_out, shard_out, sems):
        at = pl.multiple_of((1 - info[4]) * HALF, HALF)
        copies = [
            pltpu.make_async_copy(shard.at[:, :, pl.ds(at, HALF)], shard_out, sems.at[0]),
            pltpu.make_async_copy(latent.at[:, :, :, pl.ds(at, HALF)], latent_out, sems.at[1]),
        ]
        for copy in copies:
            copy.start()
        for copy in copies:
            copy.wait()

    return pl.pallas_call(
        body,
        out_shape=[
            jax.ShapeDtypeStruct(latent.shape[:3] + (HALF,), latent.dtype),
            jax.ShapeDtypeStruct(shard.shape[:2] + (HALF,), shard.dtype),
        ],
        in_specs=[SMEM, HBM, HBM],
        out_specs=[HBM, HBM],
        scratch_shapes=[pltpu.SemaphoreType.DMA((2,))],
        compiler_params=LIMIT,
    )(info, latent, shard)


def unpack(info, latent, theirs):
    def body(info, latent, theirs, rows, last, first, stat, sems):
        core = info[4]
        at = pl.multiple_of(core * HALF, HALF)
        copies = [
            pltpu.make_async_copy(
                latent.at[:, :, :, pl.ds(at, HALF)], rows.at[:, pl.ds(2 * core, 2)], sems.at[0]
            ),
            pltpu.make_async_copy(theirs, rows.at[:, pl.ds(2 - 2 * core, 2)], sems.at[1]),
        ]
        for copy in copies:
            copy.start()
        for copy in copies:
            copy.wait()
        last[...] = rows[:, ROWS - 1 :]
        first[...] = rows[:, :1]
        group = [lax.broadcasted_iota(jnp.int32, (HALF, HALF), i) // 16 for i in range(2)]
        same = (group[0] == group[1]).astype(jnp.float32)

        def over_group(values):
            values = jnp.broadcast_to(jnp.sum(values, axis=0, keepdims=True), (8, HALF))
            return lax.dot_general(
                values, same, (((1,), (0,)), ((), ())), precision=lax.Precision.HIGHEST,
                preferred_element_type=jnp.float32,
            )[:1]

        def total(of):
            sums = None
            for frame in range(2):
                for r in range(ROWS):
                    part = of(rows[frame, r].astype(jnp.float32))
                    part = jnp.sum(part.reshape(WIDTH // 8, 8, HALF), axis=0)
                    sums = part if sums is None else sums + part
            return over_group(sums)

        mean = total(lambda v: v) / CELLS
        squares = total(lambda v: (v - mean) * (v - mean))
        stat[0:1] = mean
        stat[1:2] = squares

    edge = jax.ShapeDtypeStruct((2, 1, WIDTH, HALF), latent.dtype)
    return pl.pallas_call(
        body,
        out_shape=[
            jax.ShapeDtypeStruct((2, ROWS, WIDTH, HALF), latent.dtype), edge, edge,
            jax.ShapeDtypeStruct((2, HALF), jnp.float32),
        ],
        in_specs=[SMEM, HBM, HBM],
        out_specs=[VMEM] * 4,
        scratch_shapes=[pltpu.SemaphoreType.DMA((2,))],
        compiler_params=LIMIT,
    )(info, latent, theirs)


def border(above, rows, below):
    edge = 2 * WIDTH

    def body(above, rows, below, own, sems):
        copies = [pltpu.make_async_copy(rows, own.at[:, pl.ds(1, ROWS)], sems.at[0])]
        for frame in range(2):
            at = pl.ds(frame * WIDTH, WIDTH)
            copies.append(pltpu.make_async_copy(above.at[at], own.at[frame, 0], sems.at[1 + frame]))
            copies.append(pltpu.make_async_copy(below.at[at], own.at[frame, ROWS + 1], sems.at[3 + frame]))
        for copy in copies:
            copy.start()
        for copy in copies:
            copy.wait()

    return pl.pallas_call(
        body,
        out_shape=jax.ShapeDtypeStruct((2, ROWS + 2, WIDTH, HALF), rows.dtype),
        in_specs=[HBM] * 3,
        out_specs=HBM,
        scratch_shapes=[pltpu.SemaphoreType.DMA((5,))],
        compiler_params=LIMIT,
    )(above, rows, below)


def activate(info, stats, gain, shift, pieces):
    def body(info, stats, gain, shift, *refs):
        sources, results = refs[: len(pieces)], refs[len(pieces) :]
        for (_, ahead), source, result in zip(pieces, sources, results):
            means, squares = stats[:, 2 * ahead], stats[:, 2 * ahead + 1]
            mean = jnp.sum(means, axis=0, keepdims=True) / CHIPS
            deviation = means - mean
            variance = jnp.sum(squares / CELLS + deviation * deviation, axis=0, keepdims=True) / CHIPS
            scale = lax.rsqrt(variance + EPSILON) * gain[...]
            offset = shift[...]

            def row(i, _):
                frame, r = i // 6, lax.rem(i, 6)
                v = (source[frame, r].astype(jnp.float32) - mean) * scale + offset
                s = v / (1.0 + jnp.exp(-v))
                inside = jnp.logical_and(
                    jnp.logical_or(r != 0, info[2] == 0), jnp.logical_or(r != 5, info[3] == 0)
                )
                result[frame, r] = jnp.where(inside, s, 0.0).astype(jnp.bfloat16)
                return 0

            lax.fori_loop(0, 6 * source.shape[0], row, 0, unroll=2)

    arrays = [a for a, _ in pieces]
    cells = sum(a.size for a in arrays)
    return pl.pallas_call(
        body,
        out_shape=[jax.ShapeDtypeStruct(a.shape, a.dtype) for a in arrays],
        in_specs=[SMEM] + [VMEM] * (3 + len(arrays)),
        out_specs=[VMEM] * len(arrays),
        compiler_params=LIMIT,
        cost_estimate=pl.CostEstimate(flops=16 * cells, bytes_accessed=4 * cells, transcendentals=2 * cells),
    )(info, stats, gain, shift, *arrays)


def convolve(info, bias, act, chunks, order, params):
    sizes = [len(piece) for piece in act]
    outs = 2 if len(order) > 1 else 3

    def body(info, bias, *refs):
        pieces, at = [], 0
        offset = bias[0:1, pl.ds(pl.multiple_of(info[0] * OUTS, OUTS), OUTS)]
        for size in sizes:
            piece = refs[at : at + size]
            pieces.append([(piece[0], 0), (piece[0], 1)] if size == 1 else [(piece[0], 0), (piece[1], 0)])
            at += size
        taps, (keep, *give) = refs[at:-outs], refs[-outs:]
        column = lax.broadcasted_iota(jnp.int32, (1, WIDTH, OUTS), 1)

        def matrix(tap):
            rows = [c[tap] for c in taps[:4]]
            rows.append(jnp.concatenate([taps[4][tap], taps[5][tap]], 1))
            return jnp.concatenate(rows + [c[tap] for c in taps[6:]], 0)

        def hand(slot, t, value):
            if outs == 2:
                give[0][slot, t] = value.astype(jnp.bfloat16)
            else:
                give[t][...] = value.astype(jnp.bfloat16)

        def run(slot, frames):
            for t in range(2):
                total = None
                for a in range(3):
                    ref, at = frames[t + a]
                    for b in range(3):
                        lhs = ref[at, b : b + ROWS].reshape(ROWS * WIDTH, HALF)
                        rhs = jnp.concatenate([matrix((a * 3 + b) * 3 + c) for c in range(3)], 0)
                        term = lax.dot_general(
                            lhs, rhs, (((1,), (1,)), ((), ())), preferred_element_type=jnp.float32
                        )
                        total = term if total is None else total + term
                total = total.reshape(ROWS, WIDTH, 3 * OUTS)
                left, middle, right = (total[..., c * OUTS : (c + 1) * OUTS] for c in range(3))
                left = jnp.where(column == 0, 0.0, pltpu.roll(left, 1, 1))
                right = jnp.where(column == WIDTH - 1, 0.0, pltpu.roll(right, WIDTH - 1, 1))
                total = pltpu.roll((left + middle + right).reshape(ROWS * WIDTH, OUTS), info[1], 1)
                total = total.reshape(ROWS, WIDTH, OUTS)

                @pl.when(info[4] == 0)
                def _():
                    keep[slot, t] = total[:2] + offset
                    hand(slot, t, total[2:])

                @pl.when(info[4] == 1)
                def _():
                    keep[slot, t] = total[2:] + offset
                    hand(slot, t, total[:2])

        for slot, ahead in enumerate(order):
            now, before = pieces[ahead], pieces[ahead - 1]
            span = lax.rem(info[0] + ahead, NY)

            @pl.when(span == 0)
            def _():
                run(slot, [now[0], now[0]] + now)

            @pl.when(span != 0)
            def _():
                run(slot, before + now)

    shape = (len(order), 2, 2, WIDTH, OUTS)
    arrays = [a for piece in act for a in piece]
    return pl.pallas_call(
        body,
        out_shape=[jax.ShapeDtypeStruct(shape, jnp.float32)]
        + [jax.ShapeDtypeStruct(shape if outs == 2 else shape[2:], jnp.bfloat16)] * (outs - 1),
        in_specs=[SMEM, VMEM] + [VMEM] * (len(arrays) + len(chunks)),
        out_specs=[VMEM] * outs,
        compiler_params=params,
        cost_estimate=pl.CostEstimate(
            flops=len(order) * 2 * 1024 * HALF * 27 * OUTS, bytes_accessed=5 * 2**20, transcendentals=0
        ),
    )(info, bias, *arrays, *chunks)


def mix(keep, taken):
    count = keep.shape[0]

    def body(keep, taken, *outs):
        for k in range(count):
            outs[k][...] = (keep[k] + taken[k].astype(jnp.float32)).astype(jnp.bfloat16)

    return pl.pallas_call(
        body, out_shape=[jax.ShapeDtypeStruct(taken.shape[1:], jnp.bfloat16)] * count,
        in_specs=[VMEM, VMEM], out_specs=[VMEM] * count, compiler_params=LIMIT,
    )(keep, taken)


def assemble(info, keep, taken, quarters):
    def body(info, keep, first, second, *refs):
        out = refs[-1]
        for k in range(NY):
            at = pl.multiple_of(lax.rem(info[0] + k, NY) * OUTS, OUTS)
            if k == 0:
                for t, taken in enumerate((first, second)):
                    value = keep[0, t] + taken[...].astype(jnp.float32)
                    out[t, :, :, pl.ds(at, OUTS)] = value.astype(jnp.bfloat16)
            else:
                out[:, :, :, pl.ds(at, OUTS)] = refs[k - 1][...]

    return pl.pallas_call(
        body,
        out_shape=jax.ShapeDtypeStruct((2, 2, WIDTH, NY * OUTS), jnp.bfloat16),
        in_specs=[SMEM] + [VMEM] * (NY + 2),
        out_specs=VMEM,
        compiler_params=LIMIT,
    )(info, keep, *taken, *quarters)


def per_device(latent, kernel, norm_gain, norm_shift, conv_bias):
    time_index, plane, x_index, core = (lax.axis_index(a) for a in AXES)
    chip = plane * NX + x_index
    channels = latent.shape[3]
    turn = 4 * ((chip + CHIPS - 1) % CHIPS)
    info = jnp.stack([time_index, turn, chip == 0, chip == CHIPS - 1, core]).astype(jnp.int32)
    half = lambda a: lax.dynamic_slice_in_dim(a, core * HALF, HALF, axis=a.ndim - 1)

    shard = kernel.transpose(1, 2, 3, 0, 4).reshape(TAPS, 2, channels)
    latent_give, shard_give = pack(info, latent, shard)
    other = send(shard_give, sibling)
    theirs = send(latent_give, sibling)

    near = half(shard)
    pair = jnp.where(core == 0, jnp.concatenate([near, other], 1), jnp.concatenate([other, near], 1))
    rows, last, first, stat = unpack(info, latent, theirs)
    flat = pair.reshape(TAPS * 4, HALF)
    edge = 2 * WIDTH
    from_above = send(jnp.concatenate([last.reshape(edge, HALF), flat]), strip(1))
    from_below = send(jnp.concatenate([first.reshape(edge, HALF), flat]), strip(-1))
    from_second = send(pair, strip(-2))
    block = jnp.concatenate(
        [from_above[edge:].reshape(TAPS, 4, HALF), pair, from_below[edge:].reshape(TAPS, 4, HALF), from_second], 1
    )
    own = border(from_above, rows, from_below)

    spans = [stat] + [send(stat, along_y(-k)) for k in range(1, NY)]
    spans = jnp.concatenate(spans, 0)
    spans, block, own = lax.optimization_barrier((spans, block, own))
    stats = lax.all_to_all(jnp.broadcast_to(spans[None], (CHIPS, 2 * NY, HALF)), ("z", "x"), 0, 0)

    ring = {0: block}
    for by in range(1, 4):
        ring[by] = send(ring[by - 1], along_z(-1))
        ring[-by] = send(ring[1 - by], along_z(1))
    after = send(own, along_y(-1))
    before = send(own, along_y(1))
    across_a = send(after[:1], along_y(-1))
    across_b = send(before[1:], along_y(1))

    gain, shift = half(norm_gain[None]), half(norm_shift[None])
    act_own, act_after, act_before = activate(info, stats, gain, shift, [(own, 0), (after, 1), (before, 3)])
    third, minus_third, act_own, act_after, act_before = lax.optimization_barrier(
        (ring[3], ring[-3], act_own, act_after, act_before)
    )
    far_a = send(third[..., :WIDTH], along_z(-1))
    far_b = send(minus_third[..., WIDTH:], along_z(1))
    chunks = [ring[0], ring[1], ring[2], ring[3], far_a, far_b, ring[-3], ring[-2], ring[-1]]
    act_a, act_b = activate(info, stats, gain, shift, [(across_a, 2), (across_b, 2)])
    act = [[act_own], [act_after], [act_a, act_b], [act_before]]
    order = (2, 1, 3)
    bias = conv_bias[None]
    keep, give = convolve(info, bias, act, chunks, order, LIMIT)
    mixed = mix(keep, send(give, sibling))
    quarters = [None] * NY
    late, *mixed = lax.optimization_barrier((info, *mixed))
    for slot, ahead in enumerate(order):
        quarters[-ahead] = send(mixed[slot], along_y(ahead))
    keep_own, *give_own = convolve(late, bias, act, chunks, (0,), LIMIT)
    return assemble(info, keep_own, [send(a, sibling) for a in give_own], quarters[1:])


def solution(mesh):
    mesh = Mesh(mesh.devices.reshape(NY, NZ, NX, NC), AXES)
    return jax.shard_map(
        per_device,
        mesh=mesh,
        in_specs=(
            P("y", ("z", "x", "core"), None, None),
            P(AXES, None, None, None, None),
            P(),
            P(),
            P(),
        ),
        out_specs=P("y", ("z", "x", "core"), None, None),
        check_vma=False,
    )
```

```python
import jax
import jax.numpy as jnp
from jax import lax
from jax.experimental import pallas as pl
from jax.experimental.pallas import tpu as pltpu
from jax.sharding import Mesh, PartitionSpec as P

GROUPS = 32
EPSILON = 1e-06
NY, NZ, NX, NC = 4, 8, 4, 2
CHIPS = NZ * NX
TAPS = 27

AXES = ("y", "z", "x", "core")
FRAMES, ROWS, WIDTH, HALF, OUTS = 8, 4, 128, 256, 128
CELLS = 2 * ROWS * WIDTH * 16
VMEM = pl.BlockSpec(memory_space=pltpu.VMEM)
HBM = pl.BlockSpec(memory_space=pltpu.HBM)
SMEM = pl.BlockSpec(memory_space=pltpu.SMEM)
LIMIT = pltpu.CompilerParams(vmem_limit_bytes=14 * 2**20)
WIDE = pltpu.CompilerParams(vmem_limit_bytes=60 * 2**20)


def send(array, move):
    pairs = []
    for y in range(NY):
        for z in range(NZ):
            for x in range(NX):
                for c in range(NC):
                    to = move(y, z, x, c)
                    if to is not None:
                        ty, tz, tx, tc = to
                        source = ((y * NZ + z) * NX + x) * NC + c
                        target = ((ty % NY * NZ + tz % NZ) * NX + tx % NX) * NC + tc % NC
                        pairs.append((source, target))
    return lax.ppermute(array, AXES, pairs)


def along_y(by):
    return lambda y, z, x, c: (y + by, z, x, c)


def across_y(bit):
    return lambda y, z, x, c: (y ^ bit, z, x, c)


def along_z(by):
    return lambda y, z, x, c: (y, z + by, x, c)


def along_x(by):
    return lambda y, z, x, c: (y, z, x + by, c)


def sibling(y, z, x, c):
    return (y, z, x, 1 - c)


def strip(by):
    def move(y, z, x, c):
        chip = (z * NX + x + by) % CHIPS
        return (y, chip // NX, chip % NX, c)

    return move


def unpack(info, latent, theirs):
    def body(info, latent, theirs, rows, last, first, sems):
        core = info[4]
        at = pl.multiple_of(core * HALF, HALF)
        copies = [
            pltpu.make_async_copy(
                latent.at[:, :, :, pl.ds(at, HALF)], rows.at[:, pl.ds(2 * core, 2)], sems.at[0]
            ),
            pltpu.make_async_copy(theirs, rows.at[:, pl.ds(2 - 2 * core, 2)], sems.at[1]),
        ]
        for copy in copies:
            copy.start()
        for copy in copies:
            copy.wait()
        last[...] = rows[:, ROWS - 1 :]
        first[...] = rows[:, :1]

    edge = jax.ShapeDtypeStruct((2, 1, WIDTH, HALF), latent.dtype)
    return pl.pallas_call(
        body,
        out_shape=[jax.ShapeDtypeStruct((2, ROWS, WIDTH, HALF), latent.dtype), edge, edge],
        in_specs=[SMEM, HBM, HBM],
        out_specs=[VMEM] * 3,
        scratch_shapes=[pltpu.SemaphoreType.DMA((2,))],
        compiler_params=LIMIT,
    )(info, latent, theirs)


def moments(rows):
    def body(rows, stat):
        group = [lax.broadcasted_iota(jnp.int32, (HALF, HALF), i) // 16 for i in range(2)]
        same = (group[0] == group[1]).astype(jnp.float32)

        def over_group(values):
            values = jnp.broadcast_to(jnp.sum(values, axis=0, keepdims=True), (8, HALF))
            return lax.dot_general(
                values, same, (((1,), (0,)), ((), ())), precision=lax.Precision.HIGHEST,
                preferred_element_type=jnp.float32,
            )[:1]

        def total(of):
            sums = None
            for frame in range(2):
                for r in range(ROWS):
                    part = of(rows[frame, r].astype(jnp.float32))
                    part = jnp.sum(part.reshape(WIDTH // 8, 8, HALF), axis=0)
                    sums = part if sums is None else sums + part
            return over_group(sums)

        mean = total(lambda v: v) / CELLS
        squares = total(lambda v: (v - mean) * (v - mean))
        stat[0:1] = mean
        stat[1:2] = squares

    return pl.pallas_call(
        body,
        out_shape=jax.ShapeDtypeStruct((2, HALF), jnp.float32),
        in_specs=[VMEM],
        out_specs=VMEM,
        compiler_params=LIMIT,
    )(rows)


def border(above, rows, below):
    edge = 2 * WIDTH

    def body(above, rows, below, own, sems):
        copies = [pltpu.make_async_copy(rows, own.at[:, pl.ds(1, ROWS)], sems.at[0])]
        for frame in range(2):
            at = pl.ds(frame * WIDTH, WIDTH)
            copies.append(pltpu.make_async_copy(above.at[at], own.at[frame, 0], sems.at[1 + frame]))
            copies.append(pltpu.make_async_copy(below.at[at], own.at[frame, ROWS + 1], sems.at[3 + frame]))
        for copy in copies:
            copy.start()
        for copy in copies:
            copy.wait()

    return pl.pallas_call(
        body,
        out_shape=jax.ShapeDtypeStruct((2, ROWS + 2, WIDTH, HALF), rows.dtype),
        in_specs=[HBM] * 3,
        out_specs=HBM,
        scratch_shapes=[pltpu.SemaphoreType.DMA((5,))],
        compiler_params=LIMIT,
    )(above, rows, below)


def activate(info, stats, gain, shift, pieces):
    def body(info, stats, gain, shift, *refs):
        sources, results = refs[: len(pieces)], refs[len(pieces) :]
        for (_, ahead), source, result in zip(pieces, sources, results):
            even = lax.rem(info[0], 2) == 0
            behind = (NY - ahead) % NY
            means = jnp.where(even, stats[:, 2 * ahead], stats[:, 2 * behind])
            squares = jnp.where(even, stats[:, 2 * ahead + 1], stats[:, 2 * behind + 1])
            mean = jnp.sum(means, axis=0, keepdims=True) / CHIPS
            deviation = means - mean
            variance = jnp.sum(squares / CELLS + deviation * deviation, axis=0, keepdims=True) / CHIPS
            scale = lax.rsqrt(variance + EPSILON) * gain[...]
            offset = shift[...]

            def row(i, _):
                frame, r = i // 6, lax.rem(i, 6)
                v = (source[frame, r].astype(jnp.float32) - mean) * scale + offset
                s = v / (1.0 + jnp.exp(-v))
                inside = jnp.logical_and(
                    jnp.logical_or(r != 0, info[2] == 0), jnp.logical_or(r != 5, info[3] == 0)
                )
                result[frame, r] = jnp.where(inside, s, 0.0).astype(jnp.bfloat16)
                return 0

            lax.fori_loop(0, 6 * source.shape[0], row, 0, unroll=2)

    arrays = [a for a, _ in pieces]
    cells = sum(a.size for a in arrays)
    return pl.pallas_call(
        body,
        out_shape=[jax.ShapeDtypeStruct(a.shape, a.dtype) for a in arrays],
        in_specs=[SMEM] + [VMEM] * (3 + len(arrays)),
        out_specs=[VMEM] * len(arrays),
        compiler_params=LIMIT,
        cost_estimate=pl.CostEstimate(flops=16 * cells, bytes_accessed=4 * cells, transcendentals=2 * cells),
    )(info, stats, gain, shift, *arrays)


def convolve(info, bias, act, chunks, order, params):
    sizes = [len(piece) for piece in act]
    outs = 2 if len(order) > 1 else 3

    def body(info, bias, *refs):
        pieces, at = [], 0
        offset = bias[0:1, pl.ds(pl.multiple_of(info[0] * OUTS, OUTS), OUTS)]
        for size in sizes:
            piece = refs[at : at + size]
            pieces.append([(piece[0], 0), (piece[0], 1)] if size == 1 else [(piece[0], 0), (piece[1], 0)])
            at += size
        taps, (keep, *give) = refs[at:-outs], refs[-outs:]
        column = lax.broadcasted_iota(jnp.int32, (1, WIDTH, OUTS), 1)

        def matrix(tap):
            rows = [c[tap] for c in taps[:4]]
            rows.append(jnp.concatenate([taps[4][tap], taps[5][tap]], 1))
            return jnp.concatenate(rows + [c[tap] for c in taps[6:]], 0)

        def hand(slot, t, value):
            if outs == 2:
                give[0][slot, t] = value.astype(jnp.bfloat16)
            else:
                give[t][...] = value.astype(jnp.bfloat16)

        def run(slot, frames):
            for t in range(2):
                total = None
                for a in range(3):
                    ref, at = frames[t + a]
                    for b in range(3):
                        lhs = ref[at, b : b + ROWS].reshape(ROWS * WIDTH, HALF)
                        rhs = jnp.concatenate([matrix((a * 3 + b) * 3 + c) for c in range(3)], 0)
                        term = lax.dot_general(
                            lhs, rhs, (((1,), (1,)), ((), ())), preferred_element_type=jnp.float32
                        )
                        total = term if total is None else total + term
                total = total.reshape(ROWS, WIDTH, 3 * OUTS)
                left, middle, right = (total[..., c * OUTS : (c + 1) * OUTS] for c in range(3))
                left = jnp.where(column == 0, 0.0, pltpu.roll(left, 1, 1))
                right = jnp.where(column == WIDTH - 1, 0.0, pltpu.roll(right, WIDTH - 1, 1))
                total = pltpu.roll((left + middle + right).reshape(ROWS * WIDTH, OUTS), info[1], 1)
                total = total.reshape(ROWS, WIDTH, OUTS)

                @pl.when(info[4] == 0)
                def _():
                    keep[slot, t] = total[:2] + offset
                    hand(slot, t, total[2:])

                @pl.when(info[4] == 1)
                def _():
                    keep[slot, t] = total[2:] + offset
                    hand(slot, t, total[:2])

        for slot, ahead in enumerate(order):
            now, before = pieces[ahead], pieces[ahead - 1]
            span = lax.rem(info[0] + ahead, NY)

            @pl.when(span == 0)
            def _():
                run(slot, [now[0], now[0]] + now)

            @pl.when(span != 0)
            def _():
                run(slot, before + now)

    shape = (len(order), 2, 2, WIDTH, OUTS)
    arrays = [a for piece in act for a in piece]
    return pl.pallas_call(
        body,
        out_shape=[jax.ShapeDtypeStruct(shape, jnp.float32)]
        + [jax.ShapeDtypeStruct(shape if outs == 2 else shape[2:], jnp.bfloat16)] * (outs - 1),
        in_specs=[SMEM, VMEM] + [VMEM] * (len(arrays) + len(chunks)),
        out_specs=[VMEM] * outs,
        compiler_params=params,
        cost_estimate=pl.CostEstimate(
            flops=len(order) * 2 * 1024 * HALF * 27 * OUTS, bytes_accessed=5 * 2**20, transcendentals=0
        ),
    )(info, bias, *arrays, *chunks)


def mix(keep, taken):
    count = keep.shape[0]

    def body(keep, taken, *outs):
        for k in range(count):
            outs[k][...] = (keep[k] + taken[k].astype(jnp.float32)).astype(jnp.bfloat16)

    return pl.pallas_call(
        body, out_shape=[jax.ShapeDtypeStruct(taken.shape[1:], jnp.bfloat16)] * count,
        in_specs=[VMEM, VMEM], out_specs=[VMEM] * count, compiler_params=LIMIT,
    )(keep, taken)


def assemble(info, keep, taken, quarters):
    def body(info, keep, first, second, *refs):
        out = refs[-1]
        for k in range(NY):
            at = pl.multiple_of(lax.rem(info[0] + k, NY) * OUTS, OUTS)
            if k == 0:
                for t, taken in enumerate((first, second)):
                    value = keep[0, t] + taken[...].astype(jnp.float32)
                    out[t, :, :, pl.ds(at, OUTS)] = value.astype(jnp.bfloat16)
            else:
                out[:, :, :, pl.ds(at, OUTS)] = refs[k - 1][...]

    return pl.pallas_call(
        body,
        out_shape=jax.ShapeDtypeStruct((2, 2, WIDTH, NY * OUTS), jnp.bfloat16),
        in_specs=[SMEM] + [VMEM] * (NY + 2),
        out_specs=VMEM,
        compiler_params=LIMIT,
    )(info, keep, *taken, *quarters)


def per_device(latent, kernel, norm_gain, norm_shift, conv_bias):
    time_index, plane, x_index, core = (lax.axis_index(a) for a in AXES)
    chip = plane * NX + x_index
    channels = latent.shape[3]
    turn = 4 * ((chip + CHIPS - 1) % CHIPS)
    info = jnp.stack([time_index, turn, chip == 0, chip == CHIPS - 1, core]).astype(jnp.int32)
    half = lambda a, which: lax.dynamic_slice_in_dim(a, which * HALF, HALF, axis=a.ndim - 1)

    shard = kernel.transpose(1, 2, 3, 0, 4).reshape(TAPS, 2, channels)
    other = send(half(shard, 1 - core), sibling)
    theirs = send(half(latent, 1 - core), sibling)

    near = half(shard, core)
    pair = jnp.where(core == 0, jnp.concatenate([near, other], 1), jnp.concatenate([other, near], 1))
    rows, last, first = unpack(info, latent, theirs)
    stat = moments(rows)
    flat = pair.reshape(TAPS * 4, HALF)
    edge = 2 * WIDTH
    from_above = send(jnp.concatenate([last.reshape(edge, HALF), flat]), strip(1))
    from_below = send(jnp.concatenate([first.reshape(edge, HALF), flat]), strip(-1))
    from_second = send(pair, strip(-2))
    block = jnp.concatenate(
        [from_above[edge:].reshape(TAPS, 4, HALF), pair, from_below[edge:].reshape(TAPS, 4, HALF), from_second], 1
    )
    own = border(from_above, rows, from_below)

    spans = jnp.concatenate([stat, send(stat, across_y(1))], 0)
    spans = jnp.concatenate([spans, send(spans, across_y(2))], 0)
    spans, block, own = lax.optimization_barrier((spans, block, own))
    stats = lax.all_to_all(jnp.broadcast_to(spans[None], (CHIPS, 2 * NY, HALF)), ("z", "x"), 0, 0)

    ring = {0: block}
    for by in range(1, 4):
        ring[by] = send(ring[by - 1], along_z(-1))
        ring[-by] = send(ring[1 - by], along_z(1))
    after = send(own, along_y(-1))
    before = send(own, along_y(1))
    across_a = send(after[:1], along_y(-1))
    across_b = send(before[1:], along_y(1))

    gain, shift = half(norm_gain[None], core), half(norm_shift[None], core)
    act_own, act_after, act_before = activate(info, stats, gain, shift, [(own, 0), (after, 1), (before, 3)])
    third, minus_third, act_own, act_after, act_before = lax.optimization_barrier(
        (ring[3], ring[-3], act_own, act_after, act_before)
    )
    far_a = send(third[..., :WIDTH], along_z(-1))
    far_b = send(minus_third[..., WIDTH:], along_z(1))
    chunks = [ring[0], ring[1], ring[2], ring[3], far_a, far_b, ring[-3], ring[-2], ring[-1]]
    act_a, act_b = activate(info, stats, gain, shift, [(across_a, 2), (across_b, 2)])
    act = [[act_own], [act_after], [act_a, act_b], [act_before]]
    order = (2, 1, 3)
    bias = conv_bias[None]
    keep, give = convolve(info, bias, act, chunks, order, LIMIT)
    mixed = mix(keep, send(give, sibling))
    quarters = [None] * NY
    late, *mixed = lax.optimization_barrier((info, *mixed))
    for slot, ahead in enumerate(order):
        quarters[-ahead] = send(mixed[slot], along_y(ahead))
    keep_own, *give_own = convolve(late, bias, act, chunks, (0,), LIMIT)
    return assemble(info, keep_own, [send(a, sibling) for a in give_own], quarters[1:])


def solution(mesh):
    mesh = Mesh(mesh.devices.reshape(NY, NZ, NX, NC), AXES)
    return jax.shard_map(
        per_device,
        mesh=mesh,
        in_specs=(
            P("y", ("z", "x", "core"), None, None),
            P(AXES, None, None, None, None),
            P(),
            P(),
            P(),
        ),
        out_specs=P("y", ("z", "x", "core"), None, None),
        check_vma=False,
    )
```

```python
import jax
import jax.numpy as jnp
from jax import lax
from jax.experimental import pallas as pl
from jax.experimental.pallas import tpu as pltpu
from jax.sharding import Mesh, PartitionSpec as P

GROUPS = 32
EPSILON = 1e-06
NY, NZ, NX, NC = 4, 8, 4, 2
CHIPS = NZ * NX
TAPS = 27

AXES = ("y", "z", "x", "core")
FRAMES, ROWS, WIDTH, HALF, OUTS = 8, 4, 128, 256, 128
CELLS = 2 * ROWS * WIDTH * 16
VMEM = pl.BlockSpec(memory_space=pltpu.VMEM)
HBM = pl.BlockSpec(memory_space=pltpu.HBM)
SMEM = pl.BlockSpec(memory_space=pltpu.SMEM)
LIMIT = pltpu.CompilerParams(vmem_limit_bytes=14 * 2**20)
WIDE = pltpu.CompilerParams(vmem_limit_bytes=60 * 2**20)


def send(array, move):
    pairs = []
    for y in range(NY):
        for z in range(NZ):
            for x in range(NX):
                for c in range(NC):
                    to = move(y, z, x, c)
                    if to is not None:
                        ty, tz, tx, tc = to
                        source = ((y * NZ + z) * NX + x) * NC + c
                        target = ((ty % NY * NZ + tz % NZ) * NX + tx % NX) * NC + tc % NC
                        pairs.append((source, target))
    return lax.ppermute(array, AXES, pairs)


def along_y(by):
    return lambda y, z, x, c: (y + by, z, x, c)


def across_y(bit):
    return lambda y, z, x, c: (y ^ bit, z, x, c)


def along_z(by):
    return lambda y, z, x, c: (y, z + by, x, c)


def along_x(by):
    return lambda y, z, x, c: (y, z, x + by, c)


def sibling(y, z, x, c):
    return (y, z, x, 1 - c)


def strip(by):
    def move(y, z, x, c):
        chip = (z * NX + x + by) % CHIPS
        return (y, chip // NX, chip % NX, c)

    return move


def unpack(info, latent, theirs):
    def body(info, latent, theirs, rows, last, first, sems):
        core = info[4]
        at = pl.multiple_of(core * HALF, HALF)
        copies = [
            pltpu.make_async_copy(
                latent.at[:, :, :, pl.ds(at, HALF)], rows.at[:, pl.ds(2 * core, 2)], sems.at[0]
            ),
            pltpu.make_async_copy(theirs, rows.at[:, pl.ds(2 - 2 * core, 2)], sems.at[1]),
        ]
        for copy in copies:
            copy.start()
        for copy in copies:
            copy.wait()
        last[...] = rows[:, ROWS - 1 :]
        first[...] = rows[:, :1]

    edge = jax.ShapeDtypeStruct((2, 1, WIDTH, HALF), latent.dtype)
    return pl.pallas_call(
        body,
        out_shape=[jax.ShapeDtypeStruct((2, ROWS, WIDTH, HALF), latent.dtype), edge, edge],
        in_specs=[SMEM, HBM, HBM],
        out_specs=[VMEM] * 3,
        scratch_shapes=[pltpu.SemaphoreType.DMA((2,))],
        compiler_params=LIMIT,
    )(info, latent, theirs)


def moments(rows):
    def body(rows, stat):
        group = [lax.broadcasted_iota(jnp.int32, (HALF, HALF), i) // 16 for i in range(2)]
        same = (group[0] == group[1]).astype(jnp.float32)

        def over_group(values):
            values = jnp.broadcast_to(jnp.sum(values, axis=0, keepdims=True), (8, HALF))
            return lax.dot_general(
                values, same, (((1,), (0,)), ((), ())), precision=lax.Precision.HIGHEST,
                preferred_element_type=jnp.float32,
            )[:1]

        def total(of):
            sums = None
            for frame in range(2):
                for r in range(ROWS):
                    part = of(rows[frame, r].astype(jnp.float32))
                    part = jnp.sum(part.reshape(WIDTH // 8, 8, HALF), axis=0)
                    sums = part if sums is None else sums + part
            return over_group(sums)

        mean = total(lambda v: v) / CELLS
        squares = total(lambda v: (v - mean) * (v - mean))
        stat[0:1] = mean
        stat[1:2] = squares

    return pl.pallas_call(
        body,
        out_shape=jax.ShapeDtypeStruct((2, HALF), jnp.float32),
        in_specs=[VMEM],
        out_specs=VMEM,
        compiler_params=LIMIT,
    )(rows)


def border(above, rows, below):
    edge = 2 * WIDTH

    def body(above, rows, below, own, sems):
        copies = [pltpu.make_async_copy(rows, own.at[:, pl.ds(1, ROWS)], sems.at[0])]
        for frame in range(2):
            at = pl.ds(frame * WIDTH, WIDTH)
            copies.append(pltpu.make_async_copy(above.at[at], own.at[frame, 0], sems.at[1 + frame]))
            copies.append(pltpu.make_async_copy(below.at[at], own.at[frame, ROWS + 1], sems.at[3 + frame]))
        for copy in copies:
            copy.start()
        for copy in copies:
            copy.wait()

    return pl.pallas_call(
        body,
        out_shape=jax.ShapeDtypeStruct((2, ROWS + 2, WIDTH, HALF), rows.dtype),
        in_specs=[HBM] * 3,
        out_specs=HBM,
        scratch_shapes=[pltpu.SemaphoreType.DMA((5,))],
        compiler_params=LIMIT,
    )(above, rows, below)


def activate(info, stats, gain, shift, pieces):
    def body(info, stats, gain, shift, *refs):
        sources, results = refs[: len(pieces)], refs[len(pieces) :]
        for (_, ahead), source, result in zip(pieces, sources, results):
            even = lax.rem(info[0], 2) == 0
            behind = (NY - ahead) % NY
            means = jnp.where(even, stats[:, 2 * ahead], stats[:, 2 * behind])
            squares = jnp.where(even, stats[:, 2 * ahead + 1], stats[:, 2 * behind + 1])
            mean = jnp.sum(means, axis=0, keepdims=True) / CHIPS
            deviation = means - mean
            variance = jnp.sum(squares / CELLS + deviation * deviation, axis=0, keepdims=True) / CHIPS
            scale = lax.rsqrt(variance + EPSILON) * gain[...]
            offset = shift[...]

            def row(i, _):
                frame, r = i // 6, lax.rem(i, 6)
                v = (source[frame, r].astype(jnp.float32) - mean) * scale + offset
                s = v / (1.0 + jnp.exp(-v))
                inside = jnp.logical_and(
                    jnp.logical_or(r != 0, info[2] == 0), jnp.logical_or(r != 5, info[3] == 0)
                )
                result[frame, r] = jnp.where(inside, s, 0.0).astype(jnp.bfloat16)
                return 0

            lax.fori_loop(0, 6 * source.shape[0], row, 0, unroll=2)

    arrays = [a for a, _ in pieces]
    cells = sum(a.size for a in arrays)
    return pl.pallas_call(
        body,
        out_shape=[jax.ShapeDtypeStruct(a.shape, a.dtype) for a in arrays],
        in_specs=[SMEM] + [VMEM] * (3 + len(arrays)),
        out_specs=[VMEM] * len(arrays),
        compiler_params=LIMIT,
        cost_estimate=pl.CostEstimate(flops=16 * cells, bytes_accessed=4 * cells, transcendentals=2 * cells),
    )(info, stats, gain, shift, *arrays)


def convolve(info, bias, act, chunks, order, params):
    sizes = [len(piece) for piece in act]
    outs = 2 if len(order) > 1 else 3

    def body(info, bias, *refs):
        pieces, at = [], 0
        offset = bias[0:1, pl.ds(pl.multiple_of(info[0] * OUTS, OUTS), OUTS)]
        for size in sizes:
            piece = refs[at : at + size]
            pieces.append([(piece[0], 0), (piece[0], 1)] if size == 1 else [(piece[0], 0), (piece[1], 0)])
            at += size
        taps, (keep, *give) = refs[at:-outs], refs[-outs:]
        column = lax.broadcasted_iota(jnp.int32, (1, WIDTH, OUTS), 1)

        def matrix(tap):
            rows = [c[tap] for c in taps[:4]]
            rows.append(jnp.concatenate([taps[4][tap], taps[5][tap]], 1))
            return jnp.concatenate(rows + [c[tap] for c in taps[6:]], 0)

        def hand(slot, t, value):
            if outs == 2:
                give[0][slot, t] = value.astype(jnp.bfloat16)
            else:
                give[t][...] = value.astype(jnp.bfloat16)

        def run(slot, frames):
            for t in range(2):
                total = None
                for a in range(3):
                    ref, at = frames[t + a]
                    for b in range(3):
                        lhs = ref[at, b : b + ROWS].reshape(ROWS * WIDTH, HALF)
                        rhs = jnp.concatenate([matrix((a * 3 + b) * 3 + c) for c in range(3)], 0)
                        term = lax.dot_general(
                            lhs, rhs, (((1,), (1,)), ((), ())), preferred_element_type=jnp.float32
                        )
                        total = term if total is None else total + term
                total = total.reshape(ROWS, WIDTH, 3 * OUTS)
                left, middle, right = (total[..., c * OUTS : (c + 1) * OUTS] for c in range(3))
                left = jnp.where(column == 0, 0.0, pltpu.roll(left, 1, 1))
                right = jnp.where(column == WIDTH - 1, 0.0, pltpu.roll(right, WIDTH - 1, 1))
                total = pltpu.roll((left + middle + right).reshape(ROWS * WIDTH, OUTS), info[1], 1)
                total = total.reshape(ROWS, WIDTH, OUTS)

                @pl.when(info[4] == 0)
                def _():
                    keep[slot, t] = total[:2] + offset
                    hand(slot, t, total[2:])

                @pl.when(info[4] == 1)
                def _():
                    keep[slot, t] = total[2:] + offset
                    hand(slot, t, total[:2])

        for slot, ahead in enumerate(order):
            now, before = pieces[ahead], pieces[ahead - 1]
            span = lax.rem(info[0] + ahead, NY)

            @pl.when(span == 0)
            def _():
                run(slot, [now[0], now[0]] + now)

            @pl.when(span != 0)
            def _():
                run(slot, before + now)

    shape = (len(order), 2, 2, WIDTH, OUTS)
    arrays = [a for piece in act for a in piece]
    return pl.pallas_call(
        body,
        out_shape=[jax.ShapeDtypeStruct(shape, jnp.float32)]
        + [jax.ShapeDtypeStruct(shape if outs == 2 else shape[2:], jnp.bfloat16)] * (outs - 1),
        in_specs=[SMEM, VMEM] + [VMEM] * (len(arrays) + len(chunks)),
        out_specs=[VMEM] * outs,
        compiler_params=params,
        cost_estimate=pl.CostEstimate(
            flops=len(order) * 2 * 1024 * HALF * 27 * OUTS, bytes_accessed=5 * 2**20, transcendentals=0
        ),
    )(info, bias, *arrays, *chunks)


def mix(keep, taken):
    count = keep.shape[0]

    def body(keep, taken, *outs):
        for k in range(count):
            outs[k][...] = (keep[k] + taken[k].astype(jnp.float32)).astype(jnp.bfloat16)

    return pl.pallas_call(
        body, out_shape=[jax.ShapeDtypeStruct(taken.shape[1:], jnp.bfloat16)] * count,
        in_specs=[VMEM, VMEM], out_specs=[VMEM] * count, compiler_params=LIMIT,
    )(keep, taken)


def assemble(info, keep, taken, quarters):
    def body(info, keep, first, second, *refs):
        out = refs[-1]
        for k in range(NY):
            at = pl.multiple_of(lax.rem(info[0] + k, NY) * OUTS, OUTS)
            if k == 0:
                for t, taken in enumerate((first, second)):
                    value = keep[0, t] + taken[...].astype(jnp.float32)
                    out[t, :, :, pl.ds(at, OUTS)] = value.astype(jnp.bfloat16)
            else:
                out[:, :, :, pl.ds(at, OUTS)] = refs[k - 1][...]

    return pl.pallas_call(
        body,
        out_shape=jax.ShapeDtypeStruct((2, 2, WIDTH, NY * OUTS), jnp.bfloat16),
        in_specs=[SMEM] + [VMEM] * (NY + 2),
        out_specs=VMEM,
        compiler_params=LIMIT,
    )(info, keep, *taken, *quarters)


def per_device(latent, kernel, norm_gain, norm_shift, conv_bias):
    time_index, plane, x_index, core = (lax.axis_index(a) for a in AXES)
    chip = plane * NX + x_index
    channels = latent.shape[3]
    turn = 4 * ((chip + CHIPS - 1) % CHIPS)
    info = jnp.stack([time_index, turn, chip == 0, chip == CHIPS - 1, core]).astype(jnp.int32)
    half = lambda a, which: lax.dynamic_slice_in_dim(a, which * HALF, HALF, axis=a.ndim - 1)

    shard = kernel.transpose(1, 2, 3, 0, 4).reshape(TAPS, 2, channels)
    give = half(latent, 1 - core)
    give, shard = lax.optimization_barrier((give, shard))
    theirs = send(give, sibling)
    other = half(send(shard, sibling), core)

    near = half(shard, core)
    pair = jnp.where(core == 0, jnp.concatenate([near, other], 1), jnp.concatenate([other, near], 1))
    rows, last, first = unpack(info, latent, theirs)
    stat = moments(rows)
    flat = pair.reshape(TAPS * 4, HALF)
    edge = 2 * WIDTH
    from_above = send(jnp.concatenate([last.reshape(edge, HALF), flat]), strip(1))
    from_below = send(jnp.concatenate([first.reshape(edge, HALF), flat]), strip(-1))
    from_second = send(pair, strip(-2))
    block = jnp.concatenate(
        [from_above[edge:].reshape(TAPS, 4, HALF), pair, from_below[edge:].reshape(TAPS, 4, HALF), from_second], 1
    )
    own = border(from_above, rows, from_below)

    spans = jnp.concatenate([stat, send(stat, across_y(1))], 0)
    spans = jnp.concatenate([spans, send(spans, across_y(2))], 0)
    spans, block, own = lax.optimization_barrier((spans, block, own))
    stats = lax.all_to_all(jnp.broadcast_to(spans[None], (CHIPS, 2 * NY, HALF)), ("z", "x"), 0, 0)

    ring = {0: block}
    for by in range(1, 4):
        ring[by] = send(ring[by - 1], along_z(-1))
        ring[-by] = send(ring[1 - by], along_z(1))
    after = send(own, along_y(-1))
    before = send(own, along_y(1))
    across_a = send(after[:1], along_y(-1))
    across_b = send(before[1:], along_y(1))

    gain, shift = half(norm_gain[None], core), half(norm_shift[None], core)
    act_own, act_after, act_before = activate(info, stats, gain, shift, [(own, 0), (after, 1), (before, 3)])
    third, minus_third, act_own, act_after, act_before = lax.optimization_barrier(
        (ring[3], ring[-3], act_own, act_after, act_before)
    )
    far_a = send(third[..., :WIDTH], along_z(-1))
    far_b = send(minus_third[..., WIDTH:], along_z(1))
    chunks = [ring[0], ring[1], ring[2], ring[3], far_a, far_b, ring[-3], ring[-2], ring[-1]]
    act_a, act_b = activate(info, stats, gain, shift, [(across_a, 2), (across_b, 2)])
    act = [[act_own], [act_after], [act_a, act_b], [act_before]]
    order = (2, 1, 3)
    bias = conv_bias[None]
    keep, give = convolve(info, bias, act, chunks, order, LIMIT)
    mixed = mix(keep, send(give, sibling))
    quarters = [None] * NY
    late, *mixed = lax.optimization_barrier((info, *mixed))
    for slot, ahead in enumerate(order):
        quarters[-ahead] = send(mixed[slot], along_y(ahead))
    keep_own, *give_own = convolve(late, bias, act, chunks, (0,), LIMIT)
    return assemble(info, keep_own, [send(a, sibling) for a in give_own], quarters[1:])


def solution(mesh):
    mesh = Mesh(mesh.devices.reshape(NY, NZ, NX, NC), AXES)
    return jax.shard_map(
        per_device,
        mesh=mesh,
        in_specs=(
            P("y", ("z", "x", "core"), None, None),
            P(AXES, None, None, None, None),
            P(),
            P(),
            P(),
        ),
        out_specs=P("y", ("z", "x", "core"), None, None),
        check_vma=False,
    )
```

```python
import jax
import jax.numpy as jnp
from jax import lax
from jax.experimental import pallas as pl
from jax.experimental.pallas import tpu as pltpu
from jax.sharding import Mesh, PartitionSpec as P

GROUPS = 32
EPSILON = 1e-06
NY, NZ, NX, NC = 4, 8, 4, 2
CHIPS = NZ * NX
TAPS = 27

AXES = ("y", "z", "x", "core")
FRAMES, ROWS, WIDTH, HALF, OUTS = 8, 4, 128, 256, 128
CELLS = 2 * ROWS * WIDTH * 16
VMEM = pl.BlockSpec(memory_space=pltpu.VMEM)
HBM = pl.BlockSpec(memory_space=pltpu.HBM)
SMEM = pl.BlockSpec(memory_space=pltpu.SMEM)
LIMIT = pltpu.CompilerParams(vmem_limit_bytes=14 * 2**20)
SMALL = pltpu.CompilerParams(vmem_limit_bytes=8 * 2**20)
WIDE = pltpu.CompilerParams(vmem_limit_bytes=60 * 2**20)


def send(array, move):
    pairs = []
    for y in range(NY):
        for z in range(NZ):
            for x in range(NX):
                for c in range(NC):
                    to = move(y, z, x, c)
                    if to is not None:
                        ty, tz, tx, tc = to
                        source = ((y * NZ + z) * NX + x) * NC + c
                        target = ((ty % NY * NZ + tz % NZ) * NX + tx % NX) * NC + tc % NC
                        pairs.append((source, target))
    return lax.ppermute(array, AXES, pairs)


def along_y(by):
    return lambda y, z, x, c: (y + by, z, x, c)


def across_y(bit):
    return lambda y, z, x, c: (y ^ bit, z, x, c)


def along_z(by):
    return lambda y, z, x, c: (y, z + by, x, c)


def along_x(by):
    return lambda y, z, x, c: (y, z, x + by, c)


def sibling(y, z, x, c):
    return (y, z, x, 1 - c)


def strip(by):
    def move(y, z, x, c):
        chip = (z * NX + x + by) % CHIPS
        return (y, chip // NX, chip % NX, c)

    return move


def unpack(info, latent, theirs):
    def body(info, latent, theirs, rows, last, first, sems):
        core = info[4]
        at = pl.multiple_of(core * HALF, HALF)
        copies = [
            pltpu.make_async_copy(
                latent.at[:, :, :, pl.ds(at, HALF)], rows.at[:, pl.ds(2 * core, 2)], sems.at[0]
            ),
            pltpu.make_async_copy(theirs, rows.at[:, pl.ds(2 - 2 * core, 2)], sems.at[1]),
        ]
        for copy in copies:
            copy.start()
        for copy in copies:
            copy.wait()
        last[...] = rows[:, ROWS - 1 :]
        first[...] = rows[:, :1]

    edge = jax.ShapeDtypeStruct((2, 1, WIDTH, HALF), latent.dtype)
    return pl.pallas_call(
        body,
        out_shape=[jax.ShapeDtypeStruct((2, ROWS, WIDTH, HALF), latent.dtype), edge, edge],
        in_specs=[SMEM, HBM, HBM],
        out_specs=[VMEM] * 3,
        scratch_shapes=[pltpu.SemaphoreType.DMA((2,))],
        compiler_params=SMALL,
    )(info, latent, theirs)


def moments(rows):
    def body(rows, stat):
        group = [lax.broadcasted_iota(jnp.int32, (HALF, HALF), i) // 16 for i in range(2)]
        same = (group[0] == group[1]).astype(jnp.float32)

        def over_group(values):
            values = jnp.broadcast_to(jnp.sum(values, axis=0, keepdims=True), (8, HALF))
            return lax.dot_general(
                values, same, (((1,), (0,)), ((), ())), precision=lax.Precision.HIGHEST,
                preferred_element_type=jnp.float32,
            )[:1]

        def total(of):
            sums = None
            for frame in range(2):
                for r in range(ROWS):
                    part = of(rows[frame, r].astype(jnp.float32))
                    part = jnp.sum(part.reshape(WIDTH // 8, 8, HALF), axis=0)
                    sums = part if sums is None else sums + part
            return over_group(sums)

        mean = total(lambda v: v) / CELLS
        squares = total(lambda v: (v - mean) * (v - mean))
        stat[0:1] = mean
        stat[1:2] = squares

    return pl.pallas_call(
        body,
        out_shape=jax.ShapeDtypeStruct((2, HALF), jnp.float32),
        in_specs=[VMEM],
        out_specs=VMEM,
        compiler_params=SMALL,
    )(rows)


def border(above, rows, below):
    edge = 2 * WIDTH

    def body(above, rows, below, own, sems):
        copies = [pltpu.make_async_copy(rows, own.at[:, pl.ds(1, ROWS)], sems.at[0])]
        for frame in range(2):
            at = pl.ds(frame * WIDTH, WIDTH)
            copies.append(pltpu.make_async_copy(above.at[at], own.at[frame, 0], sems.at[1 + frame]))
            copies.append(pltpu.make_async_copy(below.at[at], own.at[frame, ROWS + 1], sems.at[3 + frame]))
        for copy in copies:
            copy.start()
        for copy in copies:
            copy.wait()

    return pl.pallas_call(
        body,
        out_shape=jax.ShapeDtypeStruct((2, ROWS + 2, WIDTH, HALF), rows.dtype),
        in_specs=[HBM] * 3,
        out_specs=HBM,
        scratch_shapes=[pltpu.SemaphoreType.DMA((5,))],
        compiler_params=SMALL,
    )(above, rows, below)


def activate(info, stats, gain, shift, pieces):
    def body(info, stats, gain, shift, *refs):
        sources, results = refs[: len(pieces)], refs[len(pieces) :]
        for (_, ahead), source, result in zip(pieces, sources, results):
            even = lax.rem(info[0], 2) == 0
            behind = (NY - ahead) % NY
            means = jnp.where(even, stats[:, 2 * ahead], stats[:, 2 * behind])
            squares = jnp.where(even, stats[:, 2 * ahead + 1], stats[:, 2 * behind + 1])
            mean = jnp.sum(means, axis=0, keepdims=True) / CHIPS
            deviation = means - mean
            variance = jnp.sum(squares / CELLS + deviation * deviation, axis=0, keepdims=True) / CHIPS
            scale = lax.rsqrt(variance + EPSILON) * gain[...]
            offset = shift[...]

            def row(i, _):
                frame, r = i // 6, lax.rem(i, 6)
                v = (source[frame, r].astype(jnp.float32) - mean) * scale + offset
                s = v / (1.0 + jnp.exp(-v))
                inside = jnp.logical_and(
                    jnp.logical_or(r != 0, info[2] == 0), jnp.logical_or(r != 5, info[3] == 0)
                )
                result[frame, r] = jnp.where(inside, s, 0.0).astype(jnp.bfloat16)
                return 0

            lax.fori_loop(0, 6 * source.shape[0], row, 0, unroll=2)

    arrays = [a for a, _ in pieces]
    cells = sum(a.size for a in arrays)
    return pl.pallas_call(
        body,
        out_shape=[jax.ShapeDtypeStruct(a.shape, a.dtype) for a in arrays],
        in_specs=[SMEM] + [VMEM] * (3 + len(arrays)),
        out_specs=[VMEM] * len(arrays),
        compiler_params=SMALL,
        cost_estimate=pl.CostEstimate(flops=16 * cells, bytes_accessed=4 * cells, transcendentals=2 * cells),
    )(info, stats, gain, shift, *arrays)


def convolve(info, bias, act, chunks, order, params):
    sizes = [len(piece) for piece in act]
    outs = 2 if len(order) > 1 else 3

    def body(info, bias, *refs):
        pieces, at = [], 0
        offset = bias[0:1, pl.ds(pl.multiple_of(info[0] * OUTS, OUTS), OUTS)]
        for size in sizes:
            piece = refs[at : at + size]
            pieces.append([(piece[0], 0), (piece[0], 1)] if size == 1 else [(piece[0], 0), (piece[1], 0)])
            at += size
        taps, (keep, *give) = refs[at:-outs], refs[-outs:]
        column = lax.broadcasted_iota(jnp.int32, (1, WIDTH, OUTS), 1)

        def matrix(tap):
            rows = [c[tap] for c in taps[:4]]
            rows.append(jnp.concatenate([taps[4][tap], taps[5][tap]], 1))
            return jnp.concatenate(rows + [c[tap] for c in taps[6:]], 0)

        def hand(slot, t, value):
            if outs == 2:
                give[0][slot, t] = value.astype(jnp.bfloat16)
            else:
                give[t][...] = value.astype(jnp.bfloat16)

        def run(slot, frames):
            for t in range(2):
                total = None
                for a in range(3):
                    ref, at = frames[t + a]
                    for b in range(3):
                        lhs = ref[at, b : b + ROWS].reshape(ROWS * WIDTH, HALF)
                        rhs = jnp.concatenate([matrix((a * 3 + b) * 3 + c) for c in range(3)], 0)
                        term = lax.dot_general(
                            lhs, rhs, (((1,), (1,)), ((), ())), preferred_element_type=jnp.float32
                        )
                        total = term if total is None else total + term
                total = total.reshape(ROWS, WIDTH, 3 * OUTS)
                left, middle, right = (total[..., c * OUTS : (c + 1) * OUTS] for c in range(3))
                left = jnp.where(column == 0, 0.0, pltpu.roll(left, 1, 1))
                right = jnp.where(column == WIDTH - 1, 0.0, pltpu.roll(right, WIDTH - 1, 1))
                total = pltpu.roll((left + middle + right).reshape(ROWS * WIDTH, OUTS), info[1], 1)
                total = total.reshape(ROWS, WIDTH, OUTS)

                @pl.when(info[4] == 0)
                def _():
                    keep[slot, t] = total[:2] + offset
                    hand(slot, t, total[2:])

                @pl.when(info[4] == 1)
                def _():
                    keep[slot, t] = total[2:] + offset
                    hand(slot, t, total[:2])

        for slot, ahead in enumerate(order):
            now, before = pieces[ahead], pieces[ahead - 1]
            span = lax.rem(info[0] + ahead, NY)

            @pl.when(span == 0)
            def _():
                run(slot, [now[0], now[0]] + now)

            @pl.when(span != 0)
            def _():
                run(slot, before + now)

    shape = (len(order), 2, 2, WIDTH, OUTS)
    arrays = [a for piece in act for a in piece]
    return pl.pallas_call(
        body,
        out_shape=[jax.ShapeDtypeStruct(shape, jnp.float32)]
        + [jax.ShapeDtypeStruct(shape if outs == 2 else shape[2:], jnp.bfloat16)] * (outs - 1),
        in_specs=[SMEM, VMEM] + [VMEM] * (len(arrays) + len(chunks)),
        out_specs=[VMEM] * outs,
        compiler_params=params,
        cost_estimate=pl.CostEstimate(
            flops=len(order) * 2 * 1024 * HALF * 27 * OUTS, bytes_accessed=5 * 2**20, transcendentals=0
        ),
    )(info, bias, *arrays, *chunks)


def mix(keep, taken):
    count = keep.shape[0]

    def body(keep, taken, *outs):
        for k in range(count):
            outs[k][...] = (keep[k] + taken[k].astype(jnp.float32)).astype(jnp.bfloat16)

    return pl.pallas_call(
        body, out_shape=[jax.ShapeDtypeStruct(taken.shape[1:], jnp.bfloat16)] * count,
        in_specs=[VMEM, VMEM], out_specs=[VMEM] * count, compiler_params=SMALL,
    )(keep, taken)


def assemble(info, keep, taken, quarters):
    def body(info, keep, first, second, *refs):
        parts, out, mixed, sems = refs[: NY - 1], refs[NY - 1], refs[NY], refs[NY + 1]
        copies = []
        for k in range(NY):
            at = pl.multiple_of(lax.rem(info[0] + k, NY) * OUTS, OUTS)
            source = parts[k - 1] if k else mixed
            copies.append(pltpu.make_async_copy(source, out.at[:, :, :, pl.ds(at, OUTS)], sems.at[k]))
        for copy in copies[1:]:
            copy.start()
        for t, half in enumerate((first, second)):
            mixed[t] = (keep[0, t] + half[...].astype(jnp.float32)).astype(jnp.bfloat16)
        copies[0].start()
        for copy in copies:
            copy.wait()

    return pl.pallas_call(
        body,
        out_shape=jax.ShapeDtypeStruct((2, 2, WIDTH, NY * OUTS), jnp.bfloat16),
        in_specs=[SMEM] + [VMEM] * (NY + 2),
        out_specs=HBM,
        scratch_shapes=[pltpu.VMEM((2, 2, WIDTH, OUTS), jnp.bfloat16), pltpu.SemaphoreType.DMA((NY,))],
        compiler_params=SMALL,
    )(info, keep, *taken, *quarters)


def per_device(latent, kernel, norm_gain, norm_shift, conv_bias):
    time_index, plane, x_index, core = (lax.axis_index(a) for a in AXES)
    chip = plane * NX + x_index
    channels = latent.shape[3]
    turn = 4 * ((chip + CHIPS - 1) % CHIPS)
    info = jnp.stack([time_index, turn, chip == 0, chip == CHIPS - 1, core]).astype(jnp.int32)
    half = lambda a, which: lax.dynamic_slice_in_dim(a, which * HALF, HALF, axis=a.ndim - 1)

    shard = kernel.transpose(1, 2, 3, 0, 4).reshape(TAPS, 2, channels)
    give = half(latent, 1 - core)
    give, shard = lax.optimization_barrier((give, shard))
    theirs = send(give, sibling)
    other = half(send(shard, sibling), core)

    near = half(shard, core)
    pair = jnp.where(core == 0, jnp.concatenate([near, other], 1), jnp.concatenate([other, near], 1))
    rows, last, first = unpack(info, latent, theirs)
    stat = moments(rows)
    flat = pair.reshape(TAPS * 4, HALF)
    edge = 2 * WIDTH
    from_above = send(jnp.concatenate([last.reshape(edge, HALF), flat]), strip(1))
    from_below = send(jnp.concatenate([first.reshape(edge, HALF), flat]), strip(-1))
    from_second = send(pair, strip(-2))
    block = jnp.concatenate(
        [from_above[edge:].reshape(TAPS, 4, HALF), pair, from_below[edge:].reshape(TAPS, 4, HALF), from_second], 1
    )
    own = border(from_above, rows, from_below)

    spans = jnp.concatenate([stat, send(stat, across_y(1))], 0)
    spans = jnp.concatenate([spans, send(spans, across_y(2))], 0)
    spans, block, own = lax.optimization_barrier((spans, block, own))
    stats = lax.all_to_all(jnp.broadcast_to(spans[None], (CHIPS, 2 * NY, HALF)), ("z", "x"), 0, 0)

    ring = {0: block}
    for by in range(1, 4):
        ring[by] = send(ring[by - 1], along_z(-1))
        ring[-by] = send(ring[1 - by], along_z(1))
    after = send(own, along_y(-1))
    before = send(own, along_y(1))
    across_a = send(after[:1], along_y(-1))
    across_b = send(before[1:], along_y(1))

    gain, shift = half(norm_gain[None], core), half(norm_shift[None], core)
    act_own, act_after, act_before = activate(info, stats, gain, shift, [(own, 0), (after, 1), (before, 3)])
    third, minus_third, act_own, act_after, act_before = lax.optimization_barrier(
        (ring[3], ring[-3], act_own, act_after, act_before)
    )
    far_a = send(third[..., :WIDTH], along_z(-1))
    far_b = send(minus_third[..., WIDTH:], along_z(1))
    chunks = [ring[0], ring[1], ring[2], ring[3], far_a, far_b, ring[-3], ring[-2], ring[-1]]
    act_a, act_b = activate(info, stats, gain, shift, [(across_a, 2), (across_b, 2)])
    act = [[act_own], [act_after], [act_a, act_b], [act_before]]
    order = (2, 1, 3)
    bias = conv_bias[None]
    keep, give = convolve(info, bias, act, chunks, order, LIMIT)
    mixed = mix(keep, send(give, sibling))
    quarters = [None] * NY
    late, *mixed = lax.optimization_barrier((info, *mixed))
    for slot, ahead in enumerate(order):
        quarters[-ahead] = send(mixed[slot], along_y(ahead))
    keep_own, *give_own = convolve(late, bias, act, chunks, (0,), LIMIT)
    return assemble(info, keep_own, [send(a, sibling) for a in give_own], quarters[1:])


def solution(mesh):
    mesh = Mesh(mesh.devices.reshape(NY, NZ, NX, NC), AXES)
    return jax.shard_map(
        per_device,
        mesh=mesh,
        in_specs=(
            P("y", ("z", "x", "core"), None, None),
            P(AXES, None, None, None, None),
            P(),
            P(),
            P(),
        ),
        out_specs=P("y", ("z", "x", "core"), None, None),
        check_vma=False,
    )
```
